768 devices in a mesh: outer: 12 (over z_lo, core), inner: 64 (over z_hi, x, y).
Axes of the slice: x: 4, y: 8, z: 12 (z_hi: 2, z_lo: 6; z = z_hi * 6 + z_lo), core: 2. Of those that a mesh axis runs over, the one named last changes fastest.
Arguments:
- image_emb: float32 [196608, 1152], P(('outer', 'inner')), may hold values from -0.17677669 to 0.17677669
- text_emb: float32 [196608, 1152], P(('outer', 'inner')), may hold values from -0.17677669 to 0.17677669
- score_scale: float32 [1], replicated, may hold values from 4 to 16
- logit_bias: float32 [1], replicated, may hold values from -4 to -1
Outputs:
- grad_image: float32 [196608, 1152], P(('outer', 'inner'))
- grad_text: float32 [196608, 1152], P(('outer', 'inner'))
- row_loss: float32 [196608], P(('outer', 'inner'))
The draws below stay inside these ranges and needn't reach their ends.
All inputs are finite; a program needn't handle non-finite values.
Results may differ from the reference program's by a relative error of at most 0.0042.
Values may be sent and summed in bfloat16 or wider, within the bound.
A program may use at most 32 MiB of HBM per device.

```python
import math
import jax
import jax.numpy as jnp
from jax import lax

D = 1152
ROWS = 256
INNER_STEPS = 2
OUTER_STEPS = 2
ROWS_ALL = 196608
N_OUTER = 12
N_INNER = 64


def block_levels(stream_key, shape, shards, smallest, top_value):
    loudness = 1.0
    for axis_at, parts in shards:
        draws = jax.random.uniform(jax.random.fold_in(jax.random.fold_in(stream_key, 6), axis_at), (parts,), jnp.float32, smallest / len(shards), top_value / len(shards))
        loudness = loudness * jnp.repeat(jnp.exp(draws), shape[axis_at] // parts).reshape((-1,) + (1,) * (len(shape) - 1 - axis_at))
    return loudness


def gaussian(rng, dims, spread, most, shards=(), kind=jnp.bfloat16):
    entries = jax.random.normal(rng, dims, jnp.float32) * spread
    if len(shards) > 0:
        entries = block_levels(rng, dims, shards, -0.22, 0.18) * entries
    return jnp.clip(entries, min=-most, max=most).astype(kind)


def setup_inputs(seed: int = 0) -> dict:
    splits = jax.random.split(jax.random.key(seed), 5)
    return {
        "image_emb": gaussian(splits[0], (ROWS_ALL, D), (D ** -0.5), 0.17677669, ((0, 768),), jnp.float32),
        "text_emb": gaussian(splits[1], (ROWS_ALL, D), (D ** -0.5), 0.17677669, ((0, 768),), jnp.float32),
        "score_scale": jnp.clip(jnp.exp(jax.random.uniform(splits[2], (1,), jnp.float32, math.log(4.0), math.log(16.0))), 4.0, 16.0),
        "logit_bias": jnp.clip(jax.random.uniform(splits[3], (1,), jnp.float32, -4.0, -1.0), -4.0, -1.0),
    }


def device_meeting_step(picture_band_part, caption_band_part, sharpness_scale, rotation_steps, matching_couples):
    picture_whole_rows = picture_band_part.astype(jnp.float32)
    caption_whole_rows = caption_band_part.astype(jnp.float32)
    score_grid = sharpness_scale * jnp.dot(picture_whole_rows, caption_whole_rows.T, precision=lax.Precision.HIGHEST) + rotation_steps
    if matching_couples:
        desired_signs = jnp.eye(ROWS, dtype=jnp.float32)
    else:
        desired_signs = jnp.zeros_like(score_grid)
    loss_values = jax.nn.softplus((1.0 - 2.0 * desired_signs) * score_grid)
    coefficient_grid = (sharpness_scale * (jax.nn.sigmoid(score_grid) - desired_signs)).astype(jnp.bfloat16)
    coefficient_grid = lax.optimization_barrier(coefficient_grid).astype(jnp.float32)
    image_part = jnp.dot(coefficient_grid, caption_whole_rows, precision=lax.Precision.HIGHEST)
    text_part = jnp.dot(coefficient_grid.T, picture_whole_rows, precision=lax.Precision.HIGHEST)
    return image_part, text_part, jnp.sum(loss_values, axis=1)


def reference(image_emb, text_emb, score_scale, logit_bias):
    sharpness_scale = score_scale[0]
    rotation_steps = logit_bias[0]
    blocks = N_OUTER * N_INNER
    picture_split_rows = image_emb.astype(jnp.bfloat16).reshape(blocks, ROWS, D)
    text_bf = text_emb.astype(jnp.bfloat16).reshape(N_OUTER, N_INNER, ROWS, D)
    grad_image = jnp.zeros((blocks, ROWS, D), jnp.float32)
    grad_text = jnp.zeros((N_OUTER, N_INNER, ROWS, D), jnp.float32)
    loss_total = jnp.zeros((blocks, ROWS), jnp.float32)
    for outer_step in range(OUTER_STEPS):
        for inner_step in range(INNER_STEPS):
            met = jnp.roll(text_bf, (outer_step, inner_step), (0, 1)).reshape(blocks, ROWS, D)
            matching_couples = outer_step == 0 and inner_step == 0

            def one_block(band_parts):
                return device_meeting_step(band_parts[0], band_parts[1], sharpness_scale, rotation_steps, matching_couples)

            image_part, text_part, loss_part = lax.map(one_block, (picture_split_rows, met))
            grad_image = grad_image + image_part
            loss_total = loss_total + loss_part
            text_part = text_part.reshape(N_OUTER, N_INNER, ROWS, D)
            grad_text = grad_text + jnp.roll(text_part, (-outer_step, -inner_step), (0, 1))
    row_loss = loss_total / (OUTER_STEPS * INNER_STEPS * ROWS)
    return grad_image.reshape(ROWS_ALL, D), grad_text.reshape(ROWS_ALL, D), row_loss.reshape(ROWS_ALL)
```

```python
import functools

import jax
import jax.numpy as jnp
from jax import lax
from jax.experimental import pallas as pl
from jax.experimental.pallas import tpu as pltpu
from jax.sharding import PartitionSpec as P

INNER_STEPS = 2
OUTER_STEPS = 2
MESH = pl.DeviceIdType.MESH

CHUNKS = 4
PIECES = 16
UNITS = 2

TEXT_ROUTE = (24, 16, 8, 7, 24, 16, 8, 15, 24, 16, 8, 25, 31, 23, 25, 17)
IMAGE_ROUTE = tuple(31 - column for column in TEXT_ROUTE)


def either(*conditions):
    return functools.reduce(jnp.logical_or, conditions)


def kernel(
    scale_ref, bias_ref, image_hbm, text_hbm, grad_image_hbm, grad_text_hbm, loss_ref,
    image_f32, text_f32, own_image, own_text, images, texts, relay_image, relay_text,
    acc_image, acc_text, load_sem, store_sem, send_sem, relay_send_image, relay_send_text,
    recv_image, recv_text, recv_relay_image, recv_relay_text,
):
    outer, inner = lax.axis_index("outer"), lax.axis_index("inner")
    n_outer, n_inner = lax.axis_size("outer"), lax.axis_size("inner")
    half_size = n_inner // 2
    last = half_size - 1
    rows, width = own_image.shape
    chunk, piece, unit = rows // CHUNKS, rows // PIECES, rows // UNITS
    per_chunk = PIECES // CHUNKS

    half, column = lax.div(inner, half_size), lax.rem(inner, half_size)
    first_core = lax.rem(outer, 2) == 0
    is_last, is_first = column == last, column == 0
    not_last, not_first = column != last, column != 0
    here, there = half * half_size, (1 - half) * half_size
    up = (outer, lax.rem(inner + 1, n_inner))
    down = (outer, lax.rem(inner + n_inner - 1, n_inner))
    ahead = (lax.rem(outer + 1, n_outer), inner)
    behind = (lax.rem(outer + n_outer - 1, n_outer), inner)

    text_columns = sorted(set(TEXT_ROUTE))
    image_columns = sorted(set(IMAGE_ROUTE))

    loads = []
    for c in range(CHUNKS):
        part = pl.ds(c * chunk, chunk)
        for k, (source, target) in enumerate(((text_hbm, text_f32), (image_hbm, image_f32))):
            load = pltpu.make_async_copy(source.at[part], target.at[part], load_sem.at[k, c])
            load.start()
            loads.append(load)

    barrier = pltpu.get_barrier_semaphore()

    def greet(device):
        pl.semaphore_signal(barrier, inc=1, device_id=device, device_id_type=MESH)

    greet(ahead)
    greet(behind)

    @pl.when(not_last)
    def _():
        greet(up)

    @pl.when(not_first)
    def _():
        greet(down)

    @pl.when(is_last)
    def _():
        for c in image_columns:
            greet((outer, there + c))

    @pl.when(is_first)
    def _():
        for c in text_columns:
            greet((outer, there + c))

    relays_text = either(*[column == c for c in text_columns if c != last])
    relays_image = either(*[column == c for c in image_columns if c != 0])

    @pl.when(relays_text)
    def _():
        greet((outer, here + last))

    @pl.when(relays_image)
    def _():
        greet((outer, here))

    def as_rows(k, c):
        loads[2 * c + k].wait()
        part = pl.ds(c * chunk, chunk)
        if k == 0:
            own_text[part] = text_f32[part].astype(jnp.bfloat16)
        else:
            own_image[part] = image_f32[part].astype(jnp.bfloat16)

    as_rows(0, 0)
    as_rows(1, 0)

    peers = {}
    for c in range(half_size):
        count = 2 + (c != last) + (c != 0)
        count += len(text_columns) if c == last else c in text_columns
        count += len(image_columns) if c == 0 else c in image_columns
        peers.setdefault(count, []).append(c)
    for count, columns in peers.items():

        @pl.when(either(*[column == c for c in columns]))
        def _():
            pl.semaphore_wait(barrier, count)

    def send(source, target, sent, received, device):
        pltpu.make_async_remote_copy(
            src_ref=source, dst_ref=target, send_sem=sent, recv_sem=received,
            device_id=device, device_id_type=MESH,
        ).start()

    def arrived(target, received):
        pltpu.make_async_remote_copy(
            src_ref=target, dst_ref=target, send_sem=send_sem.at[0], recv_sem=received,
            device_id=ahead, device_id_type=MESH,
        ).wait_recv()

    def left(source, sent):
        pltpu.make_async_remote_copy(
            src_ref=source, dst_ref=source, send_sem=sent, recv_sem=recv_text.at[0, 0],
            device_id=ahead, device_id_type=MESH,
        ).wait_send()

    for c in range(CHUNKS):
        part = pl.ds(c * chunk, chunk)
        if c > 0:
            as_rows(0, c)
        send(own_text.at[part], texts.at[0, part], send_sem.at[0], recv_text.at[0, c], ahead)

        @pl.when(not_last)
        def _():
            send(own_text.at[part], texts.at[1, part], send_sem.at[1], recv_text.at[1, c], up)

        @pl.when(is_last)
        def _():
            for p in range(c * per_chunk, (c + 1) * per_chunk):
                bit = pl.ds(p * piece, piece)
                via = TEXT_ROUTE[p]
                if via == last:
                    send(own_text.at[bit], texts.at[1, bit], send_sem.at[1], recv_text.at[1, c], (outer, there))
                else:
                    send(own_text.at[bit], relay_text.at[bit], send_sem.at[1], recv_relay_text.at[p],
                         (outer, here + via))

        if c > 0:
            as_rows(1, c)
        send(own_image.at[part], images.at[0, part], send_sem.at[2], recv_image.at[0, c], behind)

        @pl.when(not_first)
        def _():
            send(own_image.at[part], images.at[1, part], send_sem.at[3], recv_image.at[1, c], down)

        @pl.when(is_first)
        def _():
            for p in range(c * per_chunk, (c + 1) * per_chunk):
                bit = pl.ds(p * piece, piece)
                via = IMAGE_ROUTE[p]
                if via == 0:
                    send(own_image.at[bit], images.at[1, bit], send_sem.at[3], recv_image.at[1, c],
                         (outer, there + last))
                else:
                    send(own_image.at[bit], relay_image.at[bit], send_sem.at[3], recv_relay_image.at[p],
                         (outer, here + via))

    scale, bias = scale_ref[0], bias_ref[0]
    tiles = [pl.ds(k * (width // 3), width // 3) for k in range(3)]

    def logits(mine, theirs):
        return scale * lax.dot_general(
            mine, theirs, (((1,), (1,)), ((), ())), preferred_element_type=jnp.float32
        ) + bias

    def sigmoid_and_tail(score):
        small = jnp.exp(-jnp.abs(score))
        share = 1.0 / (1.0 + small)
        return jnp.where(score >= 0, share, small * share), small

    def add_image(theirs, target, start):
        score = logits(own_image[...], theirs)
        positive, small = sigmoid_and_tail(score)
        if target:
            row = lax.broadcasted_iota(jnp.int32, score.shape, 0)
            col = lax.broadcasted_iota(jnp.int32, score.shape, 1) + start
            wanted = row == col
            positive = jnp.where(wanted, positive - 1.0, positive)
            score = jnp.where(wanted, -score, score)
        weights = (scale * positive).astype(jnp.bfloat16)
        loss = jnp.sum(jnp.maximum(score, 0.0) + jnp.log1p(small), axis=1, keepdims=True)
        return weights, loss

    def add_text(theirs, target, start):
        score = logits(own_text[...], theirs)
        positive, _ = sigmoid_and_tail(score)
        if target:
            row = lax.broadcasted_iota(jnp.int32, score.shape, 0)
            col = lax.broadcasted_iota(jnp.int32, score.shape, 1) + start
            positive = jnp.where(row == col, positive - 1.0, positive)
        return (scale * positive).astype(jnp.bfloat16)

    def meet_text(block, u, losses, target=False, fresh=False):
        part = pl.ds(u * unit, unit)
        weights, loss = add_image(block[part], target, u * unit)
        for tile in tiles:
            term = jnp.dot(weights, block[part, tile], preferred_element_type=jnp.float32)
            acc_image[:, tile] = term if fresh else acc_image[:, tile] + term
        return losses + loss

    def meet_image(block, u, target=False, fresh=False):
        part = pl.ds(u * unit, unit)
        weights = add_text(block[part], target, u * unit)
        for tile in tiles:
            term = jnp.dot(weights, block[part, tile], preferred_element_type=jnp.float32)
            acc_text[:, tile] = term if fresh else acc_text[:, tile] + term

    losses = jnp.zeros((rows, 1), jnp.float32)
    for u in range(UNITS):
        losses = meet_text(own_text, u, losses, target=True, fresh=u == 0)
        meet_image(own_image, u, target=True, fresh=u == 0)

    def pass_pieces(c):
        for p in range(c * per_chunk, (c + 1) * per_chunk):
            bit = pl.ds(p * piece, piece)
            if TEXT_ROUTE[p] != last:

                @pl.when(column == TEXT_ROUTE[p])
                def _():
                    arrived(relay_text.at[bit], recv_relay_text.at[p])
                    send(relay_text.at[bit], texts.at[1, bit], relay_send_text.at[p], recv_text.at[1, c],
                         (outer, there))

            if IMAGE_ROUTE[p] != 0:

                @pl.when(column == IMAGE_ROUTE[p])
                def _():
                    arrived(relay_image.at[bit], recv_relay_image.at[p])
                    send(relay_image.at[bit], images.at[1, bit], relay_send_image.at[p], recv_image.at[1, c],
                         (outer, there + last))

    def pass_text(c):
        part = pl.ds(c * chunk, chunk)
        arrived(texts.at[1, part], recv_text.at[1, c])

        @pl.when(jnp.logical_or(first_core, is_first))
        def _():
            send(texts.at[1, part], texts.at[2, part], send_sem.at[6], recv_text.at[2, c], ahead)

    def pass_image(c):
        part = pl.ds(c * chunk, chunk)
        arrived(images.at[1, part], recv_image.at[1, c])

        @pl.when(jnp.logical_or(jnp.logical_not(first_core), is_last))
        def _():
            send(images.at[1, part], images.at[2, part], send_sem.at[7], recv_image.at[2, c], behind)

    per_unit = CHUNKS // UNITS
    pass_pieces(0)
    for c in range(CHUNKS):
        part = pl.ds(c * chunk, chunk)
        if c + 1 < CHUNKS:
            pass_pieces(c + 1)
        arrived(texts.at[0, part], recv_text.at[0, c])

        @pl.when(jnp.logical_and(first_core, not_last))
        def _():
            send(texts.at[0, part], texts.at[2, part], send_sem.at[4], recv_text.at[2, c], up)

        arrived(images.at[0, part], recv_image.at[0, c])

        @pl.when(jnp.logical_and(jnp.logical_not(first_core), not_first))
        def _():
            send(images.at[0, part], images.at[2, part], send_sem.at[5], recv_image.at[2, c], down)

        @pl.when(not_first)
        def _():
            pass_text(c)

        @pl.when(not_last)
        def _():
            pass_image(c)

        if (c + 1) % per_unit == 0:
            losses = meet_text(texts.at[0], c // per_unit, losses)
            meet_image(images.at[0], c // per_unit)

    for u in range(UNITS):

        @pl.when(is_first)
        def _():
            for c in range(u * per_unit, (u + 1) * per_unit):
                pass_text(c)

        @pl.when(is_last)
        def _():
            for c in range(u * per_unit, (u + 1) * per_unit):
                pass_image(c)

        losses = meet_text(texts.at[1], u, losses)
        meet_image(images.at[1], u)

    for u in range(UNITS):
        for c in range(u * per_unit, (u + 1) * per_unit):
            part = pl.ds(c * chunk, chunk)
            arrived(texts.at[2, part], recv_text.at[2, c])
        losses = meet_text(texts.at[2], u, losses)
        if u == UNITS - 1:
            stores = [pltpu.make_async_copy(acc_image, grad_image_hbm, store_sem.at[0])]
            stores[0].start()
        for c in range(u * per_unit, (u + 1) * per_unit):
            part = pl.ds(c * chunk, chunk)
            arrived(images.at[2, part], recv_image.at[2, c])
        meet_image(images.at[2], u)
    stores.append(pltpu.make_async_copy(acc_text, grad_text_hbm, store_sem.at[1]))
    stores[1].start()
    loss_ref[...] = losses / (OUTER_STEPS * INNER_STEPS * rows)

    for k, block in ((0, own_text), (1, own_text), (2, own_image), (3, own_image)):
        left(block, send_sem.at[k])

    @pl.when(jnp.logical_and(first_core, not_last))
    def _():
        left(texts.at[0], send_sem.at[4])

    @pl.when(jnp.logical_and(jnp.logical_not(first_core), not_first))
    def _():
        left(images.at[0], send_sem.at[5])

    @pl.when(jnp.logical_or(first_core, is_first))
    def _():
        left(texts.at[1], send_sem.at[6])

    @pl.when(jnp.logical_or(jnp.logical_not(first_core), is_last))
    def _():
        left(images.at[1], send_sem.at[7])

    for p in range(PIECES):
        bit = pl.ds(p * piece, piece)
        if TEXT_ROUTE[p] != last:

            @pl.when(column == TEXT_ROUTE[p])
            def _():
                left(relay_text.at[bit], relay_send_text.at[p])

        if IMAGE_ROUTE[p] != 0:

            @pl.when(column == IMAGE_ROUTE[p])
            def _():
                left(relay_image.at[bit], relay_send_image.at[p])

    for store in stores:
        store.wait()


def per_device(image_emb, text_emb, score_scale, logit_bias):
    rows, width = image_emb.shape
    smem = pl.BlockSpec(memory_space=pltpu.SMEM)
    hbm = pl.BlockSpec(memory_space=pl.ANY)
    grad = jax.ShapeDtypeStruct((rows, width), jnp.float32)
    narrow, wide = pltpu.VMEM((rows, width), jnp.bfloat16), pltpu.VMEM((rows, width), jnp.float32)
    dma = pltpu.SemaphoreType.DMA
    grad_image, grad_text, row_loss = pl.pallas_call(
        kernel,
        out_shape=(grad, grad, jax.ShapeDtypeStruct((rows, 1), jnp.float32)),
        in_specs=[smem, smem, hbm, hbm],
        out_specs=(hbm, hbm, pl.BlockSpec(memory_space=pltpu.VMEM)),
        scratch_shapes=[
            wide, wide, narrow, narrow,
            pltpu.VMEM((3, rows, width), jnp.bfloat16),
            pltpu.VMEM((3, rows, width), jnp.bfloat16),
            narrow, narrow, wide, wide,
            dma((2, CHUNKS)), dma((2,)), dma((8,)), dma((PIECES,)), dma((PIECES,)),
            dma((3, CHUNKS)), dma((3, CHUNKS)), dma((PIECES,)), dma((PIECES,)),
        ],
        compiler_params=pltpu.CompilerParams(
            collective_id=0, has_side_effects=True, vmem_limit_bytes=48 * 2**20
        ),
    )(score_scale, logit_bias, image_emb, text_emb)
    return grad_image, grad_text, row_loss[:, 0]


def solution(mesh):
    return jax.shard_map(
        per_device,
        mesh=mesh,
        in_specs=(P(("outer", "inner"), None), P(("outer", "inner"), None), P(), P()),
        out_specs=(P(("outer", "inner"), None), P(("outer", "inner"), None), P(("outer", "inner"))),
        check_vma=False,
    )
```

```python
import functools

import jax
import jax.numpy as jnp
from jax import lax
from jax.experimental import pallas as pl
from jax.experimental.pallas import tpu as pltpu
from jax.sharding import PartitionSpec as P

INNER_STEPS = 2
OUTER_STEPS = 2
MESH = pl.DeviceIdType.MESH

CHUNKS = 4
PIECES = 16
UNITS = 2

TEXT_ROUTE = (24, 16, 8, 1, 24, 16, 8, 6, 24, 16, 8, 14, 17, 9, 1, 6)
IMAGE_ROUTE = tuple(31 - column for column in TEXT_ROUTE)


def either(*conditions):
    return functools.reduce(jnp.logical_or, conditions)


def kernel(
    scale_ref, bias_ref, image_hbm, text_hbm, acc_image, acc_text, loss_ref,
    image_f32, text_f32, own_image, own_text, images, texts, relay_image, relay_text,
    pair_losses, load_sem, send_sem, relay_send_image, relay_send_text,
    recv_image, recv_text, recv_relay_image, recv_relay_text, ready_image, ready_text,
):
    outer, inner = lax.axis_index("outer"), lax.axis_index("inner")
    n_outer, n_inner = lax.axis_size("outer"), lax.axis_size("inner")
    half_size = n_inner // 2
    last = half_size - 1
    rows, width = own_image.shape
    chunk, piece, unit = rows // CHUNKS, rows // PIECES, rows // UNITS
    per_chunk = PIECES // CHUNKS

    half, column = lax.div(inner, half_size), lax.rem(inner, half_size)
    first_core = lax.rem(outer, 2) == 0
    is_last, is_first = column == last, column == 0
    not_last, not_first = column != last, column != 0
    here, there = half * half_size, (1 - half) * half_size
    up = (outer, lax.rem(inner + 1, n_inner))
    down = (outer, lax.rem(inner + n_inner - 1, n_inner))
    ahead = (lax.rem(outer + 1, n_outer), inner)
    behind = (lax.rem(outer + n_outer - 1, n_outer), inner)

    text_columns = sorted(set(TEXT_ROUTE))
    image_columns = sorted(set(IMAGE_ROUTE))

    loads = []
    for c in range(CHUNKS):
        part = pl.ds(c * chunk, chunk)
        for k, (source, target) in enumerate(((text_hbm, text_f32), (image_hbm, image_f32))):
            load = pltpu.make_async_copy(source.at[part], target.at[part], load_sem.at[k, c])
            load.start()
            loads.append(load)

    barrier = pltpu.get_barrier_semaphore()

    def greet(device):
        pl.semaphore_signal(barrier, inc=1, device_id=device, device_id_type=MESH)

    greet(ahead)
    greet(behind)

    @pl.when(not_last)
    def _():
        greet(up)

    @pl.when(not_first)
    def _():
        greet(down)

    early = half == 0
    relays_text = either(*[column == c for c in text_columns])
    relays_image = either(*[column == c for c in image_columns])

    @pl.when(jnp.logical_and(is_last, early))
    def _():
        for c in image_columns:
            greet((outer, there + c))

    @pl.when(jnp.logical_and(is_first, early))
    def _():
        for c in text_columns:
            greet((outer, there + c))

    @pl.when(relays_text)
    def _():
        greet((outer, here + last))

        @pl.when(early)
        def _():
            greet((outer, there))

    @pl.when(relays_image)
    def _():
        greet((outer, here))

        @pl.when(early)
        def _():
            greet((outer, there + last))

    def as_rows(k, c):
        loads[2 * c + k].wait()
        part = pl.ds(c * chunk, chunk)
        if k == 0:
            own_text[part] = text_f32[part].astype(jnp.bfloat16)
        else:
            own_image[part] = image_f32[part].astype(jnp.bfloat16)

    as_rows(0, 0)
    as_rows(1, 0)

    peers = {}
    for i in range(n_inner):
        late, c = divmod(i, half_size)
        count = 2 + (c != last) + (c != 0)
        count += (1 + late) * len(text_columns) if c == last else late * (c in text_columns)
        count += (1 + late) * len(image_columns) if c == 0 else late * (c in image_columns)
        peers.setdefault(count, []).append(i)
    for count, places in peers.items():

        @pl.when(either(*[inner == i for i in places]))
        def _():
            pl.semaphore_wait(barrier, count)

    @pl.when(jnp.logical_and(is_last, jnp.logical_not(early)))
    def _():
        for c in image_columns:
            pl.semaphore_signal(ready_image, inc=1, device_id=(outer, there + c), device_id_type=MESH)

    @pl.when(jnp.logical_and(is_first, jnp.logical_not(early)))
    def _():
        for c in text_columns:
            pl.semaphore_signal(ready_text, inc=1, device_id=(outer, there + c), device_id_type=MESH)

    def send(source, target, sent, received, device):
        pltpu.make_async_remote_copy(
            src_ref=source, dst_ref=target, send_sem=sent, recv_sem=received,
            device_id=device, device_id_type=MESH,
        ).start()

    def arrived(target, received):
        pltpu.make_async_remote_copy(
            src_ref=target, dst_ref=target, send_sem=send_sem.at[0], recv_sem=received,
            device_id=ahead, device_id_type=MESH,
        ).wait_recv()

    def left(source, sent):
        pltpu.make_async_remote_copy(
            src_ref=source, dst_ref=source, send_sem=sent, recv_sem=recv_text.at[0, 0],
            device_id=ahead, device_id_type=MESH,
        ).wait_send()

    for c in range(CHUNKS):
        part = pl.ds(c * chunk, chunk)
        if c > 0:
            as_rows(0, c)
        send(own_text.at[part], texts.at[0, part], send_sem.at[0], recv_text.at[0, c], ahead)

        @pl.when(not_last)
        def _():
            send(own_text.at[part], texts.at[1, part], send_sem.at[1], recv_text.at[1, c], up)

        @pl.when(is_last)
        def _():
            for p in range(c * per_chunk, (c + 1) * per_chunk):
                bit = pl.ds(p * piece, piece)
                via = TEXT_ROUTE[p]
                send(own_text.at[bit], relay_text.at[bit], send_sem.at[1], recv_relay_text.at[p],
                     (outer, here + via))

        if c > 0:
            as_rows(1, c)
        send(own_image.at[part], images.at[0, part], send_sem.at[2], recv_image.at[0, c], behind)

        @pl.when(not_first)
        def _():
            send(own_image.at[part], images.at[1, part], send_sem.at[3], recv_image.at[1, c], down)

        @pl.when(is_first)
        def _():
            for p in range(c * per_chunk, (c + 1) * per_chunk):
                bit = pl.ds(p * piece, piece)
                via = IMAGE_ROUTE[p]
                send(own_image.at[bit], relay_image.at[bit], send_sem.at[3], recv_relay_image.at[p],
                     (outer, here + via))

    @pl.when(jnp.logical_and(relays_text, early))
    def _():
        pl.semaphore_wait(ready_text, 1)

    @pl.when(jnp.logical_and(relays_image, early))
    def _():
        pl.semaphore_wait(ready_image, 1)

    for p in range(PIECES):
        c = p // per_chunk
        bit = pl.ds(p * piece, piece)

        @pl.when(column == TEXT_ROUTE[p])
        def _():
            arrived(relay_text.at[bit], recv_relay_text.at[p])
            send(relay_text.at[bit], texts.at[1, bit], relay_send_text.at[p], recv_text.at[1, c], (outer, there))

        @pl.when(column == IMAGE_ROUTE[p])
        def _():
            arrived(relay_image.at[bit], recv_relay_image.at[p])
            send(relay_image.at[bit], images.at[1, bit], relay_send_image.at[p], recv_image.at[1, c],
                 (outer, there + last))

    scale, bias = scale_ref[0], bias_ref[0]
    tiles = [pl.ds(k * (width // 3), width // 3) for k in range(3)]

    def logits(mine, theirs):
        return scale * lax.dot_general(
            mine, theirs, (((1,), (1,)), ((), ())), preferred_element_type=jnp.float32
        ) + bias

    def sigmoid_and_tail(score):
        small = jnp.exp(-jnp.abs(score))
        share = 1.0 / (1.0 + small)
        return jnp.where(score >= 0, share, small * share), small

    def add_image(theirs, target, start):
        score = logits(own_image[...], theirs)
        positive, small = sigmoid_and_tail(score)
        if target:
            row = lax.broadcasted_iota(jnp.int32, score.shape, 0)
            col = lax.broadcasted_iota(jnp.int32, score.shape, 1) + start
            wanted = row == col
            positive = jnp.where(wanted, positive - 1.0, positive)
            score = jnp.where(wanted, -score, score)
        weights = (scale * positive).astype(jnp.bfloat16)
        return weights, jnp.maximum(score, 0.0) + jnp.log1p(small)

    def add_text(theirs, target, start):
        score = logits(own_text[...], theirs)
        positive, _ = sigmoid_and_tail(score)
        if target:
            row = lax.broadcasted_iota(jnp.int32, score.shape, 0)
            col = lax.broadcasted_iota(jnp.int32, score.shape, 1) + start
            positive = jnp.where(row == col, positive - 1.0, positive)
        return (scale * positive).astype(jnp.bfloat16)

    def meet_text(block, u, target=False, fresh=False):
        part = pl.ds(u * unit, unit)
        weights, loss = add_image(block[part], target, u * unit)
        for tile in tiles:
            term = jnp.dot(weights, block[part, tile], preferred_element_type=jnp.float32)
            acc_image[:, tile] = term if fresh else acc_image[:, tile] + term
        pair_losses[...] = loss if fresh else pair_losses[...] + loss

    def meet_image(block, u, target=False, fresh=False):
        part = pl.ds(u * unit, unit)
        weights = add_text(block[part], target, u * unit)
        for tile in tiles:
            term = jnp.dot(weights, block[part, tile], preferred_element_type=jnp.float32)
            acc_text[:, tile] = term if fresh else acc_text[:, tile] + term

    for u in range(UNITS):
        meet_text(own_text, u, target=True, fresh=u == 0)
        meet_image(own_image, u, target=True, fresh=u == 0)

    def pass_text(c):
        part = pl.ds(c * chunk, chunk)
        arrived(texts.at[1, part], recv_text.at[1, c])

        @pl.when(jnp.logical_or(first_core, is_first))
        def _():
            send(texts.at[1, part], texts.at[2, part], send_sem.at[6], recv_text.at[2, c], ahead)

    def pass_image(c):
        part = pl.ds(c * chunk, chunk)
        arrived(images.at[1, part], recv_image.at[1, c])

        @pl.when(jnp.logical_or(jnp.logical_not(first_core), is_last))
        def _():
            send(images.at[1, part], images.at[2, part], send_sem.at[7], recv_image.at[2, c], behind)

    per_unit = CHUNKS // UNITS
    for c in range(CHUNKS):
        part = pl.ds(c * chunk, chunk)
        arrived(texts.at[0, part], recv_text.at[0, c])

        @pl.when(jnp.logical_and(first_core, not_last))
        def _():
            send(texts.at[0, part], texts.at[2, part], send_sem.at[4], recv_text.at[2, c], up)

        arrived(images.at[0, part], recv_image.at[0, c])

        @pl.when(jnp.logical_and(jnp.logical_not(first_core), not_first))
        def _():
            send(images.at[0, part], images.at[2, part], send_sem.at[5], recv_image.at[2, c], down)

        @pl.when(not_first)
        def _():
            pass_text(c)

        @pl.when(not_last)
        def _():
            pass_image(c)

        if (c + 1) % per_unit == 0:
            meet_text(texts.at[0], c // per_unit)
            meet_image(images.at[0], c // per_unit)

    for u in range(UNITS):

        @pl.when(is_first)
        def _():
            for c in range(u * per_unit, (u + 1) * per_unit):
                pass_text(c)

        @pl.when(is_last)
        def _():
            for c in range(u * per_unit, (u + 1) * per_unit):
                pass_image(c)

        meet_text(texts.at[1], u)
        meet_image(images.at[1], u)

    for u in range(UNITS):
        for c in range(u * per_unit, (u + 1) * per_unit):
            part = pl.ds(c * chunk, chunk)
            arrived(texts.at[2, part], recv_text.at[2, c])
        meet_text(texts.at[2], u)
        for c in range(u * per_unit, (u + 1) * per_unit):
            part = pl.ds(c * chunk, chunk)
            arrived(images.at[2, part], recv_image.at[2, c])
        meet_image(images.at[2], u)
    row_losses = jnp.sum(jnp.transpose(pair_losses[...]), axis=0, keepdims=True)
    loss_ref[...] = row_losses / (OUTER_STEPS * INNER_STEPS * rows)

    for k, block in ((0, own_text), (1, own_text), (2, own_image), (3, own_image)):
        left(block, send_sem.at[k])

    @pl.when(jnp.logical_and(first_core, not_last))
    def _():
        left(texts.at[0], send_sem.at[4])

    @pl.when(jnp.logical_and(jnp.logical_not(first_core), not_first))
    def _():
        left(images.at[0], send_sem.at[5])

    @pl.when(jnp.logical_or(first_core, is_first))
    def _():
        left(texts.at[1], send_sem.at[6])

    @pl.when(jnp.logical_or(jnp.logical_not(first_core), is_last))
    def _():
        left(images.at[1], send_sem.at[7])

    for p in range(PIECES):
        bit = pl.ds(p * piece, piece)

        @pl.when(column == TEXT_ROUTE[p])
        def _():
            left(relay_text.at[bit], relay_send_text.at[p])

        @pl.when(column == IMAGE_ROUTE[p])
        def _():
            left(relay_image.at[bit], relay_send_image.at[p])


def per_device(image_emb, text_emb, score_scale, logit_bias):
    rows, width = image_emb.shape
    smem = pl.BlockSpec(memory_space=pltpu.SMEM)
    hbm, vmem = pl.BlockSpec(memory_space=pltpu.HBM), pl.BlockSpec(memory_space=pltpu.VMEM)
    grad = jax.ShapeDtypeStruct((rows, width), jnp.float32)
    narrow, wide = pltpu.VMEM((rows, width), jnp.bfloat16), pltpu.VMEM((rows, width), jnp.float32)
    three = pltpu.VMEM((3, rows, width), jnp.bfloat16)
    dma = pltpu.SemaphoreType.DMA
    grad_image, grad_text, row_loss = pl.pallas_call(
        kernel,
        out_shape=(grad, grad, jax.ShapeDtypeStruct((1, rows), jnp.float32)),
        in_specs=[smem, smem, hbm, hbm],
        out_specs=(vmem, vmem, vmem),
        scratch_shapes=[
            wide, wide, narrow, narrow, three, three, narrow, narrow,
            pltpu.VMEM((rows, rows // UNITS), jnp.float32),
            dma((2, CHUNKS)), dma((8,)), dma((PIECES,)), dma((PIECES,)),
            dma((3, CHUNKS)), dma((3, CHUNKS)), dma((PIECES,)), dma((PIECES,)),
            pltpu.SemaphoreType.REGULAR, pltpu.SemaphoreType.REGULAR,
        ],
        compiler_params=pltpu.CompilerParams(
            collective_id=0, has_side_effects=True, vmem_limit_bytes=51 * 2**20
        ),
    )(score_scale, logit_bias, image_emb, text_emb)
    return grad_image, grad_text, row_loss[0]


def solution(mesh):
    return jax.shard_map(
        per_device,
        mesh=mesh,
        in_specs=(P(("outer", "inner"), None), P(("outer", "inner"), None), P(), P()),
        out_specs=(P(("outer", "inner"), None), P(("outer", "inner"), None), P(("outer", "inner"))),
        check_vma=False,
    )
```

```python
import functools

import jax
import jax.numpy as jnp
from jax import lax
from jax.experimental import pallas as pl
from jax.experimental.pallas import tpu as pltpu
from jax.sharding import PartitionSpec as P

INNER_STEPS = 2
OUTER_STEPS = 2
MESH = pl.DeviceIdType.MESH

CHUNKS = 4
PIECES = 16
UNITS = 2

TEXT_ROUTE = (24, 16, 8, 1, 24, 16, 8, 6, 24, 16, 8, 14, 17, 9, 1, 6)
LATE_ORDER = (0, 1, -1, -2, -3, 2, 3, -4)
ORDER = tuple(range(PIECES))
IMAGE_ROUTE = tuple(31 - column for column in TEXT_ROUTE)


def either(*conditions):
    return functools.reduce(jnp.logical_or, conditions)


def kernel(
    scale_ref, bias_ref, image_hbm, text_hbm, acc_image, acc_text, loss_ref,
    image_f32, text_f32, own_image, own_text, images, texts, relay_image, relay_text,
    pair_losses, load_sem, send_sem, relay_send_image, relay_send_text,
    recv_image, recv_text, recv_relay_image, recv_relay_text,
    recv_cross_image, recv_cross_text, ready_image, ready_text,
):
    outer, inner = lax.axis_index("outer"), lax.axis_index("inner")
    n_outer, n_inner = lax.axis_size("outer"), lax.axis_size("inner")
    half_size = n_inner // 2
    last = half_size - 1
    rows, width = own_image.shape
    chunk, piece, unit = rows // CHUNKS, rows // PIECES, rows // UNITS
    per_chunk = PIECES // CHUNKS

    half, column = lax.div(inner, half_size), lax.rem(inner, half_size)
    first_core = lax.rem(outer, 2) == 0
    is_last, is_first = column == last, column == 0
    not_last, not_first = column != last, column != 0
    here, there = half * half_size, (1 - half) * half_size
    up = (outer, lax.rem(inner + 1, n_inner))
    down = (outer, lax.rem(inner + n_inner - 1, n_inner))
    ahead = (lax.rem(outer + 1, n_outer), inner)
    behind = (lax.rem(outer + n_outer - 1, n_outer), inner)

    text_columns = sorted(set(TEXT_ROUTE))
    image_columns = sorted(set(IMAGE_ROUTE))

    loads = []
    for c in range(CHUNKS):
        part = pl.ds(c * chunk, chunk)
        for k, (source, target) in enumerate(((text_hbm, text_f32), (image_hbm, image_f32))):
            load = pltpu.make_async_copy(source.at[part], target.at[part], load_sem.at[k, c])
            load.start()
            loads.append(load)

    barrier = pltpu.get_barrier_semaphore()

    def greet(device):
        pl.semaphore_signal(barrier, inc=1, device_id=device, device_id_type=MESH)

    greet(ahead)
    greet(behind)

    @pl.when(not_last)
    def _():
        greet(up)

    @pl.when(not_first)
    def _():
        greet(down)

    early = half == 0
    relays_text = either(*[column == c for c in text_columns])
    relays_image = either(*[column == c for c in image_columns])

    @pl.when(jnp.logical_and(is_last, early))
    def _():
        for c in image_columns:
            greet((outer, there + c))

    @pl.when(jnp.logical_and(is_first, early))
    def _():
        for c in text_columns:
            greet((outer, there + c))

    @pl.when(relays_text)
    def _():
        greet((outer, here + last))

        @pl.when(early)
        def _():
            greet((outer, there))

    @pl.when(relays_image)
    def _():
        greet((outer, here))

        @pl.when(early)
        def _():
            greet((outer, there + last))

    def as_rows(k, c):
        loads[2 * c + k].wait()
        part = pl.ds(c * chunk, chunk)
        if k == 0:
            own_text[part] = text_f32[part].astype(jnp.bfloat16)
        else:
            own_image[part] = image_f32[part].astype(jnp.bfloat16)

    as_rows(0, 0)
    as_rows(1, 0)

    peers = {}
    for i in range(n_inner):
        late, c = divmod(i, half_size)
        count = 2 + (c != last) + (c != 0)
        count += (1 + late) * len(text_columns) if c == last else late * (c in text_columns)
        count += (1 + late) * len(image_columns) if c == 0 else late * (c in image_columns)
        peers.setdefault(count, []).append(i)
    for count, places in peers.items():

        @pl.when(either(*[inner == i for i in places]))
        def _():
            pl.semaphore_wait(barrier, count)

    @pl.when(jnp.logical_and(is_last, jnp.logical_not(early)))
    def _():
        for c in image_columns:
            pl.semaphore_signal(ready_image, inc=1, device_id=(outer, there + c), device_id_type=MESH)

    @pl.when(jnp.logical_and(is_first, jnp.logical_not(early)))
    def _():
        for c in text_columns:
            pl.semaphore_signal(ready_text, inc=1, device_id=(outer, there + c), device_id_type=MESH)

    def send(source, target, sent, received, device):
        pltpu.make_async_remote_copy(
            src_ref=source, dst_ref=target, send_sem=sent, recv_sem=received,
            device_id=device, device_id_type=MESH,
        ).start()

    def arrived(target, received):
        pltpu.make_async_remote_copy(
            src_ref=target, dst_ref=target, send_sem=send_sem.at[0], recv_sem=received,
            device_id=ahead, device_id_type=MESH,
        ).wait_recv()

    def left(source, sent):
        pltpu.make_async_remote_copy(
            src_ref=source, dst_ref=source, send_sem=sent, recv_sem=recv_text.at[0, 0],
            device_id=ahead, device_id_type=MESH,
        ).wait_send()

    @pl.when(is_last)
    def _():
        for p in range(PIECES):
            if p % per_chunk == 0 and p > 0:
                as_rows(0, p // per_chunk)
            bit = pl.ds(p * piece, piece)
            send(own_text.at[bit], relay_text.at[bit], send_sem.at[1], recv_relay_text.at[p],
                 (outer, here + TEXT_ROUTE[p]))

    @pl.when(is_first)
    def _():
        for p in range(PIECES):
            if p % per_chunk == 0 and p > 0:
                as_rows(1, p // per_chunk)
            bit = pl.ds(p * piece, piece)
            send(own_image.at[bit], relay_image.at[bit], send_sem.at[3], recv_relay_image.at[p],
                 (outer, here + IMAGE_ROUTE[p]))

    def send_own(c):
        part = pl.ds(c * chunk, chunk)

        @pl.when(not_last)
        def _():
            if c > 0:
                as_rows(0, c)
            send(own_text.at[part], texts.at[1, part], send_sem.at[1], recv_text.at[1, c], up)

        send(own_text.at[part], texts.at[0, part], send_sem.at[0], recv_text.at[0, c], ahead)

        @pl.when(not_first)
        def _():
            if c > 0:
                as_rows(1, c)
            send(own_image.at[part], images.at[1, part], send_sem.at[3], recv_image.at[1, c], down)

        send(own_image.at[part], images.at[0, part], send_sem.at[2], recv_image.at[0, c], behind)

    def pass_pieces(c):
        for p in range(c * per_chunk, (c + 1) * per_chunk):
            bit = pl.ds(p * piece, piece)

            @pl.when(column == TEXT_ROUTE[p])
            def _():
                arrived(relay_text.at[bit], recv_relay_text.at[p])
                send(relay_text.at[bit], texts.at[1, bit], relay_send_text.at[p], recv_cross_text.at[p],
                     (outer, there))

            @pl.when(column == IMAGE_ROUTE[p])
            def _():
                arrived(relay_image.at[bit], recv_relay_image.at[p])
                send(relay_image.at[bit], images.at[1, bit], relay_send_image.at[p], recv_cross_image.at[p],
                     (outer, there + last))

    for step in LATE_ORDER:
        if step >= 0:
            send_own(step)
        else:
            pl.when(jnp.logical_not(early))(functools.partial(pass_pieces, -1 - step))

    @pl.when(early)
    def _():
        @pl.when(relays_text)
        def _():
            pl.semaphore_wait(ready_text, 1)

        @pl.when(relays_image)
        def _():
            pl.semaphore_wait(ready_image, 1)

        for c in range(CHUNKS):
            pass_pieces(c)

    scale, bias = scale_ref[0], bias_ref[0]
    tiles = [pl.ds(k * (width // 3), width // 3) for k in range(3)]

    def logits(mine, theirs):
        return scale * lax.dot_general(
            mine, theirs, (((1,), (1,)), ((), ())), preferred_element_type=jnp.float32
        ) + bias

    def sigmoid_and_tail(score):
        small = jnp.exp(-jnp.abs(score))
        share = 1.0 / (1.0 + small)
        return jnp.where(score >= 0, share, small * share), small

    def add_image(theirs, target, start):
        score = logits(own_image[...], theirs)
        positive, small = sigmoid_and_tail(score)
        if target:
            row = lax.broadcasted_iota(jnp.int32, score.shape, 0)
            col = lax.broadcasted_iota(jnp.int32, score.shape, 1) + start
            wanted = row == col
            positive = jnp.where(wanted, positive - 1.0, positive)
            score = jnp.where(wanted, -score, score)
        weights = (scale * positive).astype(jnp.bfloat16)
        return weights, jnp.maximum(score, 0.0) + jnp.log1p(small)

    def add_text(theirs, target, start):
        score = logits(own_text[...], theirs)
        positive, _ = sigmoid_and_tail(score)
        if target:
            row = lax.broadcasted_iota(jnp.int32, score.shape, 0)
            col = lax.broadcasted_iota(jnp.int32, score.shape, 1) + start
            positive = jnp.where(row == col, positive - 1.0, positive)
        return (scale * positive).astype(jnp.bfloat16)

    def meet_text(block, u, target=False, fresh=False):
        part = pl.ds(u * unit, unit)
        weights, loss = add_image(block[part], target, u * unit)
        for tile in tiles:
            term = jnp.dot(weights, block[part, tile], preferred_element_type=jnp.float32)
            acc_image[:, tile] = term if fresh else acc_image[:, tile] + term
        pair_losses[...] = loss if fresh else pair_losses[...] + loss

    def meet_image(block, u, target=False, fresh=False):
        part = pl.ds(u * unit, unit)
        weights = add_text(block[part], target, u * unit)
        for tile in tiles:
            term = jnp.dot(weights, block[part, tile], preferred_element_type=jnp.float32)
            acc_text[:, tile] = term if fresh else acc_text[:, tile] + term

    for u in range(UNITS):
        meet_text(own_text, u, target=True, fresh=u == 0)
        meet_image(own_image, u, target=True, fresh=u == 0)

    def pass_text(c):
        part = pl.ds(c * chunk, chunk)
        arrived(texts.at[1, part], recv_text.at[1, c])

        @pl.when(first_core)
        def _():
            send(texts.at[1, part], texts.at[2, part], send_sem.at[6], recv_text.at[2, c], ahead)

    def pass_image(c):
        part = pl.ds(c * chunk, chunk)
        arrived(images.at[1, part], recv_image.at[1, c])

        @pl.when(jnp.logical_not(first_core))
        def _():
            send(images.at[1, part], images.at[2, part], send_sem.at[7], recv_image.at[2, c], behind)

    def end_text():
        for u in range(UNITS):
            for c in range(u * per_unit, (u + 1) * per_unit):
                part = pl.ds(c * chunk, chunk)
                arrived(texts.at[2, part], recv_text.at[2, c])
            meet_text(texts.at[2], u)

    def end_image():
        for u in range(UNITS):
            for c in range(u * per_unit, (u + 1) * per_unit):
                part = pl.ds(c * chunk, chunk)
                arrived(images.at[2, part], recv_image.at[2, c])
            meet_image(images.at[2], u)

    per_unit = CHUNKS // UNITS
    for c in range(CHUNKS):
        part = pl.ds(c * chunk, chunk)
        arrived(texts.at[0, part], recv_text.at[0, c])

        @pl.when(jnp.logical_and(first_core, not_last))
        def _():
            send(texts.at[0, part], texts.at[2, part], send_sem.at[4], recv_text.at[2, c], up)

        arrived(images.at[0, part], recv_image.at[0, c])

        @pl.when(jnp.logical_and(jnp.logical_not(first_core), not_first))
        def _():
            send(images.at[0, part], images.at[2, part], send_sem.at[5], recv_image.at[2, c], down)

        @pl.when(not_first)
        def _():
            pass_text(c)

        @pl.when(not_last)
        def _():
            pass_image(c)

        if (c + 1) % per_unit == 0:
            meet_text(texts.at[0], c // per_unit)
            meet_image(images.at[0], c // per_unit)

    @pl.when(not_first)
    def _():
        for u in range(UNITS):
            meet_text(texts.at[1], u)

    @pl.when(not_last)
    def _():
        for u in range(UNITS):
            meet_image(images.at[1], u)

    @pl.when(jnp.logical_and(is_first, early))
    def _():
        end_image()

    @pl.when(is_first)
    def _():
        for p in ORDER:
            bit = pl.ds(p * piece, piece)
            arrived(texts.at[1, bit], recv_cross_text.at[p])
            send(texts.at[1, bit], texts.at[2, bit], send_sem.at[6], recv_text.at[2, p // per_chunk], ahead)
        for u in range(UNITS):
            meet_text(texts.at[1], u)

    @pl.when(jnp.logical_or(not_last, jnp.logical_not(early)))
    def _():
        end_text()

    @pl.when(jnp.logical_and(is_last, early))
    def _():
        end_text()

    @pl.when(is_last)
    def _():
        for p in ORDER:
            bit = pl.ds(p * piece, piece)
            arrived(images.at[1, bit], recv_cross_image.at[p])
            send(images.at[1, bit], images.at[2, bit], send_sem.at[7], recv_image.at[2, p // per_chunk], behind)
        for u in range(UNITS):
            meet_image(images.at[1], u)

    @pl.when(jnp.logical_or(not_first, jnp.logical_not(early)))
    def _():
        end_image()

    row_losses = jnp.sum(jnp.transpose(pair_losses[...]), axis=0, keepdims=True)
    loss_ref[...] = row_losses / (OUTER_STEPS * INNER_STEPS * rows)

    for k, block in ((0, own_text), (1, own_text), (2, own_image), (3, own_image)):
        left(block, send_sem.at[k])

    @pl.when(jnp.logical_and(first_core, not_last))
    def _():
        left(texts.at[0], send_sem.at[4])

    @pl.when(jnp.logical_and(jnp.logical_not(first_core), not_first))
    def _():
        left(images.at[0], send_sem.at[5])

    @pl.when(jnp.logical_or(first_core, is_first))
    def _():
        left(texts.at[1], send_sem.at[6])

    @pl.when(jnp.logical_or(jnp.logical_not(first_core), is_last))
    def _():
        left(images.at[1], send_sem.at[7])

    for p in range(PIECES):
        bit = pl.ds(p * piece, piece)

        @pl.when(column == TEXT_ROUTE[p])
        def _():
            left(relay_text.at[bit], relay_send_text.at[p])

        @pl.when(column == IMAGE_ROUTE[p])
        def _():
            left(relay_image.at[bit], relay_send_image.at[p])


def per_device(image_emb, text_emb, score_scale, logit_bias):
    rows, width = image_emb.shape
    smem = pl.BlockSpec(memory_space=pltpu.SMEM)
    hbm, vmem = pl.BlockSpec(memory_space=pltpu.HBM), pl.BlockSpec(memory_space=pltpu.VMEM)
    grad = jax.ShapeDtypeStruct((rows, width), jnp.float32)
    narrow, wide = pltpu.VMEM((rows, width), jnp.bfloat16), pltpu.VMEM((rows, width), jnp.float32)
    three = pltpu.VMEM((3, rows, width), jnp.bfloat16)
    dma = pltpu.SemaphoreType.DMA
    grad_image, grad_text, row_loss = pl.pallas_call(
        kernel,
        out_shape=(grad, grad, jax.ShapeDtypeStruct((1, rows), jnp.float32)),
        in_specs=[smem, smem, hbm, hbm],
        out_specs=(vmem, vmem, vmem),
        scratch_shapes=[
            wide, wide, narrow, narrow, three, three, narrow, narrow,
            pltpu.VMEM((rows, rows // UNITS), jnp.float32),
            dma((2, CHUNKS)), dma((8,)), dma((PIECES,)), dma((PIECES,)),
            dma((3, CHUNKS)), dma((3, CHUNKS)), dma((PIECES,)), dma((PIECES,)),
            dma((PIECES,)), dma((PIECES,)), pltpu.SemaphoreType.REGULAR, pltpu.SemaphoreType.REGULAR,
        ],
        compiler_params=pltpu.CompilerParams(
            collective_id=0, has_side_effects=True, vmem_limit_bytes=51 * 2**20
        ),
    )(score_scale, logit_bias, image_emb, text_emb)
    return grad_image, grad_text, row_loss[0]


def solution(mesh):
    return jax.shard_map(
        per_device,
        mesh=mesh,
        in_specs=(P(("outer", "inner"), None), P(("outer", "inner"), None), P(), P()),
        out_specs=(P(("outer", "inner"), None), P(("outer", "inner"), None), P(("outer", "inner"))),
        check_vma=False,
    )
```

```python
import functools

import jax
import jax.numpy as jnp
from jax import lax
from jax.experimental import pallas as pl
from jax.experimental.pallas import tpu as pltpu
from jax.sharding import PartitionSpec as P

INNER_STEPS = 2
OUTER_STEPS = 2
MESH = pl.DeviceIdType.MESH

CHUNKS = 4
PIECES = 16
UNITS = 1

TEXT_ROUTE = (24, 16, 8, 1, 24, 16, 8, 6, 24, 16, 8, 14, 17, 9, 1, 6)
LATE_ORDER = (0, 1, -1, -2, -3, 2, 3, -4)
ORDER = tuple(range(PIECES))
IMAGE_ROUTE = tuple(31 - column for column in TEXT_ROUTE)


def either(*conditions):
    return functools.reduce(jnp.logical_or, conditions)


def kernel(
    scale_ref, bias_ref, image_hbm, text_hbm, acc_image, acc_text, loss_ref,
    image_f32, text_f32, own_image, own_text, images, texts, relay_image, relay_text,
    pair_losses, load_sem, send_sem, relay_send_image, relay_send_text,
    recv_image, recv_text, recv_relay_image, recv_relay_text,
    recv_cross_image, recv_cross_text, ready_image, ready_text,
):
    outer, inner = lax.axis_index("outer"), lax.axis_index("inner")
    n_outer, n_inner = lax.axis_size("outer"), lax.axis_size("inner")
    half_size = n_inner // 2
    last = half_size - 1
    rows, width = own_image.shape
    chunk, piece, unit = rows // CHUNKS, rows // PIECES, rows // UNITS
    per_chunk = PIECES // CHUNKS

    half, column = lax.div(inner, half_size), lax.rem(inner, half_size)
    first_core = lax.rem(outer, 2) == 0
    is_last, is_first = column == last, column == 0
    not_last, not_first = column != last, column != 0
    here, there = half * half_size, (1 - half) * half_size
    up = (outer, lax.rem(inner + 1, n_inner))
    down = (outer, lax.rem(inner + n_inner - 1, n_inner))
    ahead = (lax.rem(outer + 1, n_outer), inner)
    behind = (lax.rem(outer + n_outer - 1, n_outer), inner)

    text_columns = sorted(set(TEXT_ROUTE))
    image_columns = sorted(set(IMAGE_ROUTE))

    loads = []
    for c in range(CHUNKS):
        part = pl.ds(c * chunk, chunk)
        for k, (source, target) in enumerate(((text_hbm, text_f32), (image_hbm, image_f32))):
            load = pltpu.make_async_copy(source.at[part], target.at[part], load_sem.at[k, c])
            load.start()
            loads.append(load)

    barrier = pltpu.get_barrier_semaphore()

    def greet(device):
        pl.semaphore_signal(barrier, inc=1, device_id=device, device_id_type=MESH)

    greet(ahead)
    greet(behind)

    @pl.when(not_last)
    def _():
        greet(up)

    @pl.when(not_first)
    def _():
        greet(down)

    early = half == 0
    relays_text = either(*[column == c for c in text_columns])
    relays_image = either(*[column == c for c in image_columns])

    @pl.when(jnp.logical_and(is_last, early))
    def _():
        for c in image_columns:
            greet((outer, there + c))

    @pl.when(jnp.logical_and(is_first, early))
    def _():
        for c in text_columns:
            greet((outer, there + c))

    @pl.when(relays_text)
    def _():
        greet((outer, here + last))

        @pl.when(early)
        def _():
            greet((outer, there))

    @pl.when(relays_image)
    def _():
        greet((outer, here))

        @pl.when(early)
        def _():
            greet((outer, there + last))

    def as_rows(k, c):
        loads[2 * c + k].wait()
        part = pl.ds(c * chunk, chunk)
        if k == 0:
            own_text[part] = text_f32[part].astype(jnp.bfloat16)
        else:
            own_image[part] = image_f32[part].astype(jnp.bfloat16)

    as_rows(0, 0)
    as_rows(1, 0)

    peers = {}
    for i in range(n_inner):
        late, c = divmod(i, half_size)
        count = 2 + (c != last) + (c != 0)
        count += (1 + late) * len(text_columns) if c == last else late * (c in text_columns)
        count += (1 + late) * len(image_columns) if c == 0 else late * (c in image_columns)
        peers.setdefault(count, []).append(i)
    for count, places in peers.items():

        @pl.when(either(*[inner == i for i in places]))
        def _():
            pl.semaphore_wait(barrier, count)

    @pl.when(jnp.logical_and(is_last, jnp.logical_not(early)))
    def _():
        for c in image_columns:
            pl.semaphore_signal(ready_image, inc=1, device_id=(outer, there + c), device_id_type=MESH)

    @pl.when(jnp.logical_and(is_first, jnp.logical_not(early)))
    def _():
        for c in text_columns:
            pl.semaphore_signal(ready_text, inc=1, device_id=(outer, there + c), device_id_type=MESH)

    def send(source, target, sent, received, device):
        pltpu.make_async_remote_copy(
            src_ref=source, dst_ref=target, send_sem=sent, recv_sem=received,
            device_id=device, device_id_type=MESH,
        ).start()

    def arrived(target, received):
        pltpu.make_async_remote_copy(
            src_ref=target, dst_ref=target, send_sem=send_sem.at[0], recv_sem=received,
            device_id=ahead, device_id_type=MESH,
        ).wait_recv()

    def left(source, sent):
        pltpu.make_async_remote_copy(
            src_ref=source, dst_ref=source, send_sem=sent, recv_sem=recv_text.at[0, 0],
            device_id=ahead, device_id_type=MESH,
        ).wait_send()

    @pl.when(is_last)
    def _():
        for p in range(PIECES):
            if p % per_chunk == 0 and p > 0:
                as_rows(0, p // per_chunk)
            bit = pl.ds(p * piece, piece)
            send(own_text.at[bit], relay_text.at[bit], send_sem.at[1], recv_relay_text.at[p],
                 (outer, here + TEXT_ROUTE[p]))

    @pl.when(is_first)
    def _():
        for p in range(PIECES):
            if p % per_chunk == 0 and p > 0:
                as_rows(1, p // per_chunk)
            bit = pl.ds(p * piece, piece)
            send(own_image.at[bit], relay_image.at[bit], send_sem.at[3], recv_relay_image.at[p],
                 (outer, here + IMAGE_ROUTE[p]))

    def send_own(c):
        part = pl.ds(c * chunk, chunk)

        @pl.when(not_last)
        def _():
            if c > 0:
                as_rows(0, c)
            send(own_text.at[part], texts.at[1, part], send_sem.at[1], recv_text.at[1, c], up)

        send(own_text.at[part], texts.at[0, part], send_sem.at[0], recv_text.at[0, c], ahead)

        @pl.when(not_first)
        def _():
            if c > 0:
                as_rows(1, c)
            send(own_image.at[part], images.at[1, part], send_sem.at[3], recv_image.at[1, c], down)

        send(own_image.at[part], images.at[0, part], send_sem.at[2], recv_image.at[0, c], behind)

    def pass_pieces(c):
        for p in range(c * per_chunk, (c + 1) * per_chunk):
            bit = pl.ds(p * piece, piece)

            @pl.when(column == TEXT_ROUTE[p])
            def _():
                arrived(relay_text.at[bit], recv_relay_text.at[p])
                send(relay_text.at[bit], texts.at[1, bit], relay_send_text.at[p], recv_cross_text.at[p],
                     (outer, there))

            @pl.when(column == IMAGE_ROUTE[p])
            def _():
                arrived(relay_image.at[bit], recv_relay_image.at[p])
                send(relay_image.at[bit], images.at[1, bit], relay_send_image.at[p], recv_cross_image.at[p],
                     (outer, there + last))

    for step in LATE_ORDER:
        if step >= 0:
            send_own(step)
        else:
            pl.when(jnp.logical_not(early))(functools.partial(pass_pieces, -1 - step))

    @pl.when(early)
    def _():
        @pl.when(relays_text)
        def _():
            pl.semaphore_wait(ready_text, 1)

        @pl.when(relays_image)
        def _():
            pl.semaphore_wait(ready_image, 1)

        for c in range(CHUNKS):
            pass_pieces(c)

    scale, bias = scale_ref[0], bias_ref[0]
    tiles = [pl.ds(k * (width // 3), width // 3) for k in range(3)]

    def logits(mine, theirs):
        return scale * lax.dot_general(
            mine, theirs, (((1,), (1,)), ((), ())), preferred_element_type=jnp.float32
        ) + bias

    def sigmoid_and_tail(score):
        small = jnp.exp(-jnp.abs(score))
        share = 1.0 / (1.0 + small)
        return jnp.where(score >= 0, share, small * share), small

    def add_image(theirs, target, start):
        score = logits(own_image[...], theirs)
        positive, small = sigmoid_and_tail(score)
        if target:
            row = lax.broadcasted_iota(jnp.int32, score.shape, 0)
            col = lax.broadcasted_iota(jnp.int32, score.shape, 1) + start
            wanted = row == col
            positive = jnp.where(wanted, positive - 1.0, positive)
            score = jnp.where(wanted, -score, score)
        weights = (scale * positive).astype(jnp.bfloat16)
        return weights, jnp.maximum(score, 0.0) + jnp.log1p(small)

    def add_text(theirs, target, start):
        score = logits(own_text[...], theirs)
        positive, _ = sigmoid_and_tail(score)
        if target:
            row = lax.broadcasted_iota(jnp.int32, score.shape, 0)
            col = lax.broadcasted_iota(jnp.int32, score.shape, 1) + start
            positive = jnp.where(row == col, positive - 1.0, positive)
        return (scale * positive).astype(jnp.bfloat16)

    def meet_text(block, u, target=False, fresh=False):
        part = pl.ds(u * unit, unit)
        weights, loss = add_image(block[part], target, u * unit)
        for tile in tiles:
            term = jnp.dot(weights, block[part, tile], preferred_element_type=jnp.float32)
            acc_image[:, tile] = term if fresh else acc_image[:, tile] + term
        pair_losses[...] = loss if fresh else pair_losses[...] + loss

    def meet_image(block, u, target=False, fresh=False):
        part = pl.ds(u * unit, unit)
        weights = add_text(block[part], target, u * unit)
        for tile in tiles:
            term = jnp.dot(weights, block[part, tile], preferred_element_type=jnp.float32)
            acc_text[:, tile] = term if fresh else acc_text[:, tile] + term

    for u in range(UNITS):
        meet_text(own_text, u, target=True, fresh=u == 0)
        meet_image(own_image, u, target=True, fresh=u == 0)

    def pass_text(c):
        part = pl.ds(c * chunk, chunk)
        arrived(texts.at[1, part], recv_text.at[1, c])

        @pl.when(first_core)
        def _():
            send(texts.at[1, part], texts.at[2, part], send_sem.at[6], recv_text.at[2, c], ahead)

    def pass_image(c):
        part = pl.ds(c * chunk, chunk)
        arrived(images.at[1, part], recv_image.at[1, c])

        @pl.when(jnp.logical_not(first_core))
        def _():
            send(images.at[1, part], images.at[2, part], send_sem.at[7], recv_image.at[2, c], behind)

    def end_text():
        for u in range(UNITS):
            for c in range(u * per_unit, (u + 1) * per_unit):
                part = pl.ds(c * chunk, chunk)
                arrived(texts.at[2, part], recv_text.at[2, c])
            meet_text(texts.at[2], u)

    def end_image():
        for u in range(UNITS):
            for c in range(u * per_unit, (u + 1) * per_unit):
                part = pl.ds(c * chunk, chunk)
                arrived(images.at[2, part], recv_image.at[2, c])
            meet_image(images.at[2], u)

    per_unit = CHUNKS // UNITS
    for c in range(CHUNKS):
        part = pl.ds(c * chunk, chunk)
        arrived(texts.at[0, part], recv_text.at[0, c])

        @pl.when(jnp.logical_and(first_core, not_last))
        def _():
            send(texts.at[0, part], texts.at[2, part], send_sem.at[4], recv_text.at[2, c], up)

        arrived(images.at[0, part], recv_image.at[0, c])

        @pl.when(jnp.logical_and(jnp.logical_not(first_core), not_first))
        def _():
            send(images.at[0, part], images.at[2, part], send_sem.at[5], recv_image.at[2, c], down)

        @pl.when(not_first)
        def _():
            pass_text(c)

        @pl.when(not_last)
        def _():
            pass_image(c)

        if (c + 1) % per_unit == 0:
            meet_text(texts.at[0], c // per_unit)
            meet_image(images.at[0], c // per_unit)

    @pl.when(not_first)
    def _():
        for u in range(UNITS):
            meet_text(texts.at[1], u)

    @pl.when(not_last)
    def _():
        for u in range(UNITS):
            meet_image(images.at[1], u)

    @pl.when(jnp.logical_and(is_first, early))
    def _():
        end_image()

    @pl.when(is_first)
    def _():
        for p in ORDER:
            bit = pl.ds(p * piece, piece)
            arrived(texts.at[1, bit], recv_cross_text.at[p])
            send(texts.at[1, bit], texts.at[2, bit], send_sem.at[6], recv_text.at[2, p // per_chunk], ahead)
        for u in range(UNITS):
            meet_text(texts.at[1], u)

    @pl.when(jnp.logical_or(not_last, jnp.logical_not(early)))
    def _():
        end_text()

    @pl.when(jnp.logical_and(is_last, early))
    def _():
        end_text()

    @pl.when(is_last)
    def _():
        for p in ORDER:
            bit = pl.ds(p * piece, piece)
            arrived(images.at[1, bit], recv_cross_image.at[p])
            send(images.at[1, bit], images.at[2, bit], send_sem.at[7], recv_image.at[2, p // per_chunk], behind)
        for u in range(UNITS):
            meet_image(images.at[1], u)

    @pl.when(jnp.logical_or(not_first, jnp.logical_not(early)))
    def _():
        end_image()

    row_losses = jnp.sum(jnp.transpose(pair_losses[...]), axis=0, keepdims=True)
    loss_ref[...] = row_losses / (OUTER_STEPS * INNER_STEPS * rows)

    for k, block in ((0, own_text), (1, own_text), (2, own_image), (3, own_image)):
        left(block, send_sem.at[k])

    @pl.when(jnp.logical_and(first_core, not_last))
    def _():
        left(texts.at[0], send_sem.at[4])

    @pl.when(jnp.logical_and(jnp.logical_not(first_core), not_first))
    def _():
        left(images.at[0], send_sem.at[5])

    @pl.when(jnp.logical_or(first_core, is_first))
    def _():
        left(texts.at[1], send_sem.at[6])

    @pl.when(jnp.logical_or(jnp.logical_not(first_core), is_last))
    def _():
        left(images.at[1], send_sem.at[7])

    for p in range(PIECES):
        bit = pl.ds(p * piece, piece)

        @pl.when(column == TEXT_ROUTE[p])
        def _():
            left(relay_text.at[bit], relay_send_text.at[p])

        @pl.when(column == IMAGE_ROUTE[p])
        def _():
            left(relay_image.at[bit], relay_send_image.at[p])


def per_device(image_emb, text_emb, score_scale, logit_bias):
    rows, width = image_emb.shape
    smem = pl.BlockSpec(memory_space=pltpu.SMEM)
    hbm, vmem = pl.BlockSpec(memory_space=pltpu.HBM), pl.BlockSpec(memory_space=pltpu.VMEM)
    grad = jax.ShapeDtypeStruct((rows, width), jnp.float32)
    narrow, wide = pltpu.VMEM((rows, width), jnp.bfloat16), pltpu.VMEM((rows, width), jnp.float32)
    three = pltpu.VMEM((3, rows, width), jnp.bfloat16)
    dma = pltpu.SemaphoreType.DMA
    grad_image, grad_text, row_loss = pl.pallas_call(
        kernel,
        out_shape=(grad, grad, jax.ShapeDtypeStruct((1, rows), jnp.float32)),
        in_specs=[smem, smem, hbm, hbm],
        out_specs=(vmem, vmem, vmem),
        scratch_shapes=[
            wide, wide, narrow, narrow, three, three, narrow, narrow,
            pltpu.VMEM((rows, rows // UNITS), jnp.float32),
            dma((2, CHUNKS)), dma((8,)), dma((PIECES,)), dma((PIECES,)),
            dma((3, CHUNKS)), dma((3, CHUNKS)), dma((PIECES,)), dma((PIECES,)),
            dma((PIECES,)), dma((PIECES,)), pltpu.SemaphoreType.REGULAR, pltpu.SemaphoreType.REGULAR,
        ],
        compiler_params=pltpu.CompilerParams(
            collective_id=0, has_side_effects=True, vmem_limit_bytes=51 * 2**20
        ),
    )(score_scale, logit_bias, image_emb, text_emb)
    return grad_image, grad_text, row_loss[0]


def solution(mesh):
    return jax.shard_map(
        per_device,
        mesh=mesh,
        in_specs=(P(("outer", "inner"), None), P(("outer", "inner"), None), P(), P()),
        out_specs=(P(("outer", "inner"), None), P(("outer", "inner"), None), P(("outer", "inner"))),
        check_vma=False,
    )
```
